1024 devices in a mesh: node: 128 (over x, z, core), chip: 8 (over y).
Axes of the slice: x: 8, y: 8, z: 8, core: 2. Of those that a mesh axis runs over, the one named last changes fastest.
Arguments:
- grad_out: bfloat16 [4096, 4096], P('node', 'chip'), may hold values from -6 to 6
- route_score: bfloat16 [4096, 8], P('node'), may hold values from 0.049804688 to 0.5
- expert_routes: int32 [256, 256], P('node'), may hold values from 0 to 32767, as said below
- expert_count: int32 [256], P('node'), may hold values from 0 to 256, as said below
- gate_pre: bfloat16 [256, 256, 1024], P('node', None, 'chip'), may hold values from -6 to 6
- up_pre: bfloat16 [256, 256, 1024], P('node', None, 'chip'), may hold values from -6 to 6
- w_down: bfloat16 [256, 1024, 4096], P('node', 'chip'), may hold values from -0.1875 to 0.1875
Outputs:
- grad_gate: bfloat16 [256, 256, 1024], P('node', None, 'chip')
- grad_up: bfloat16 [256, 256, 1024], P('node', None, 'chip')
- grad_score: float32 [4096, 8], P('node')
The draws below stay inside these ranges and needn't reach their ends.
Inputs may be any that keep to these rules, and one draw needn't show every extreme that they name: `expert_routes`: the alive slots of an expert hold distinct routes in increasing order, and each route index stands in at most one alive slot; slots at or beyond expert_count hold 0. Each route names the expert that the token chose at that position; the 8 experts of a token are distinct and lie in at most 4 of the 8 groups of 32 consecutive experts. `expert_count`: some expert is full in every draw.
All inputs are finite; a program needn't handle non-finite values.
Results may differ from the reference program's by a relative error of at most 0.001.
Values may be sent and summed in bfloat16 or wider, within the bound.
A program may use at most 32 MiB of HBM per device.

```python
import math
import jax
import jax.numpy as jnp
from jax import lax

D = 4096
FF = 1024
TOP = 8
GROUPS = 8
LIMIT = 4
EXPERTS = 256
TOKENS = 4096
CAP = 256


def routing_tables(key):
    group_size = EXPERTS // GROUPS
    key_hot, key_group, key_popular, key_expert = jax.random.split(key, 4)
    hot_expert = jax.random.randint(key_hot, (), 0, EXPERTS)
    hot_group = hot_expert // group_size
    stride = max(1, TOKENS // CAP)
    forced = jnp.arange(TOKENS) % stride == 0
    group_ids = jnp.arange(GROUPS)
    group_score = jax.random.randint(key_group, (TOKENS, GROUPS), 0, 1000)
    group_score = group_score + jnp.where(forced[:, None] & (group_ids[None, :] == hot_group), 100000, 0)
    _, top_groups = lax.top_k(group_score * GROUPS + group_ids[None, :], LIMIT)
    chosen = jnp.any(group_ids[None, None, :] == top_groups[:, :, None], axis=1)
    expert_ids = jnp.arange(EXPERTS)
    allowed = chosen[:, expert_ids // group_size]
    popular = jax.random.randint(key_popular, (EXPERTS,), 0, 4) * 300
    expert_score = jax.random.randint(key_expert, (TOKENS, EXPERTS), 0, 1000) + popular[None, :]
    expert_score = expert_score + jnp.where(forced[:, None] & (expert_ids[None, :] == hot_expert), 100000, 0)
    expert_score = jnp.where(allowed, expert_score, -1000000)
    _, choices_made = lax.top_k(expert_score * EXPERTS + expert_ids[None, :], TOP)
    total_routes = TOKENS * TOP
    flat_expert = choices_made.reshape(total_routes).astype(jnp.int32)
    route_ids = jnp.arange(total_routes, dtype=jnp.int32)
    order = jnp.argsort(flat_expert * total_routes + route_ids).astype(jnp.int32)
    sorted_expert = flat_expert[order]
    full_count = jax.ops.segment_sum(jnp.ones((total_routes,), jnp.int32), flat_expert, EXPERTS)
    first_slot = jnp.cumsum(full_count) - full_count
    rank = route_ids - first_slot[sorted_expert]
    keep = rank < CAP
    table = jnp.zeros((EXPERTS, CAP), jnp.int32)
    table = table.at[jnp.where(keep, sorted_expert, EXPERTS), jnp.where(keep, rank, 0)].set(order, mode='drop')
    counts = jnp.minimum(full_count, CAP).astype(jnp.int32)
    return (table, counts)


def draw_expert_routes(key, part):
    table, counts = routing_tables(key)
    return table


def draw_expert_count(key, part):
    table, counts = routing_tables(key)
    return counts


def shard_levels(stream_key, extent, pieces, least, largest):
    factor_of = 1.0
    for dim, parts in pieces:
        draws = jax.random.uniform(jax.random.fold_in(jax.random.fold_in(stream_key, 6), dim), (parts,), jnp.float32, least / len(pieces), largest / len(pieces))
        factor_of = factor_of * jnp.repeat(jnp.exp(draws), extent[dim] // parts).reshape((-1,) + (1,) * (len(extent) - 1 - dim))
    return factor_of


def scatter_about(own_key, shape, spread, most, shards=(), held_as=jnp.bfloat16):
    entries = spread * jax.random.normal(own_key, shape, jnp.float32)
    if shards:
        entries = entries * shard_levels(own_key, shape, shards, -0.22, 0.18)
    return jnp.clip(entries, -most, most).astype(held_as)


def setup_inputs(seed: int = 0) -> dict:
    key_list = jax.random.split(jax.random.key(seed), 8)
    return {
        "grad_out": scatter_about(key_list[0], (TOKENS, D), 1.0, 6.0, ((0, 128), (1, 8))),
        "route_score": jnp.clip(jnp.exp(math.log(0.5) - 2.306499 * jax.random.uniform(key_list[1], (TOKENS, TOP), jnp.float32) ** shard_levels(key_list[1], (TOKENS, TOP), ((0, 128),), -0.2, 0.2)), 0.049804688, 0.5).astype(jnp.bfloat16),
        "expert_routes": draw_expert_routes(jax.random.fold_in(key_list[7], 71), 0),
        "expert_count": draw_expert_count(jax.random.fold_in(key_list[7], 71), 0),
        "gate_pre": scatter_about(key_list[4], (EXPERTS, CAP, FF), 1.0, 6.0, ((0, 128), (2, 8))),
        "up_pre": scatter_about(key_list[5], (EXPERTS, CAP, FF), 1.0, 6.0, ((0, 128), (2, 8))),
        "w_down": scatter_about(key_list[6], (EXPERTS, FF, D), FF ** -0.5, 0.1875, ((0, 128), (1, 8))),
    }


def reference(grad_out, route_score, expert_routes, expert_count, gate_pre, up_pre, w_down):
    slot_index = jnp.arange(CAP, dtype=jnp.int32)
    alive = slot_index[None, :] < expert_count[:, None]
    token_ids = expert_routes // TOP
    positions = expert_routes % TOP
    slot_weight = jnp.where(alive, route_score[token_ids, positions].astype(jnp.float32), jnp.float32(0.0))

    def per_expert(inputs):
        ids_row, alive_row, weight_row, gate_row, up_row, weight_matrix = inputs
        picked = jnp.where(alive_row[:, None], grad_out[ids_row], jnp.zeros((), jnp.bfloat16))
        back = jnp.dot(picked, weight_matrix.T, preferred_element_type=jnp.float32)
        pre_gate = gate_row.astype(jnp.float32)
        pre_up = up_row.astype(jnp.float32)
        sigmoid_gate = jax.nn.sigmoid(pre_gate)
        silu_gate = pre_gate * sigmoid_gate
        hidden = silu_gate * pre_up
        slot_sum = jnp.sum(hidden * back, axis=1)
        scaled_back = weight_row[:, None] * back
        alive_mask = alive_row[:, None]
        derivative = sigmoid_gate * (1.0 + pre_gate * (1.0 - sigmoid_gate))
        grad_gate = jnp.where(alive_mask, scaled_back * pre_up * derivative, jnp.float32(0.0)).astype(jnp.bfloat16)
        grad_up = jnp.where(alive_mask, scaled_back * silu_gate, jnp.float32(0.0)).astype(jnp.bfloat16)
        return grad_gate, grad_up, slot_sum

    grad_gate, grad_up, slot_sum = lax.map(per_expert, (token_ids, alive, slot_weight, gate_pre, up_pre, w_down))
    flat_term = jnp.zeros((TOKENS * TOP,), jnp.float32)
    flat_term = flat_term.at[expert_routes.reshape(-1)].add(jnp.where(alive, slot_sum, jnp.float32(0.0)).reshape(-1))
    return grad_gate, grad_up, flat_term.reshape(TOKENS, TOP)
```

```python
import functools

import jax
import jax.numpy as jnp
from jax import lax
from jax.experimental import pallas as pl
from jax.experimental.pallas import tpu as pltpu
from jax.sharding import PartitionSpec as P

LANES = 128
TOP_BITS = 3


def bits_of(size):
    return size.bit_length() - 1


def dot_f32(a, b):
    return jnp.dot(a, b, preferred_element_type=jnp.float32)


def remote(src, dst, send, recv, node, chip):
    return pltpu.make_async_remote_copy(
        src_ref=src,
        dst_ref=dst,
        send_sem=send,
        recv_sem=recv,
        device_id=(node, chip),
        device_id_type=pl.DeviceIdType.MESH,
    )


def kernel(
    n,
    ny,
    grad_ref,
    score_ref,
    routes_ref,
    count_ref,
    gate_hbm,
    up_hbm,
    w_hbm,
    grad_gate_ref,
    grad_up_ref,
    grad_score_ref,
    table,
    onehot,
    ids,
    pick_send,
    pick_recv,
    pick_own,
    picked,
    gate_buf,
    up_buf,
    w_buf,
    back,
    low_hot,
    sums,
    dense_send,
    dense_recv,
    total_buf,
    in_sem,
    ids_send_sem,
    ids_recv_sem,
    line_send,
    line_recv,
    ring_send,
    ring_recv,
    pick_send_sem,
    pick_recv_sem,
    chip_send,
    chip_recv,
    sum_send,
    sum_recv,
    dense_send_sem,
    dense_recv_sem,
    total_send,
    total_recv,
):
    chunks = table.shape[1]
    feats = chunks - 1
    tokens = table.shape[3]
    experts, cap = routes_ref.shape
    slots = experts * cap
    width = n * tokens
    half_ring, half_chip = n // 2, ny // 2
    nbits = bits_of(n)
    groups = ((0, 1), (1, chunks))

    node = lax.axis_index("node")
    chip = lax.axis_index("chip")
    core = lax.rem(node, 2)
    z = lax.rem(node // 2, n)
    x = node // (2 * n)
    line = x + core * (z - x)
    ring = z + core * (x - z)
    sibling = node + 1 - 2 * core

    def node_at(ring_pos, line_pos):
        at_x = line_pos + core * (ring_pos - line_pos)
        at_z = ring_pos + core * (line_pos - ring_pos)
        return (at_x * n + at_z) * 2 + core

    def line_peer(d):
        return lax.rem(line + d, n)

    loads = [
        pltpu.make_async_copy(w_hbm, w_buf, in_sem.at[0]),
        pltpu.make_async_copy(gate_hbm, gate_buf, in_sem.at[1]),
        pltpu.make_async_copy(up_hbm, up_buf, in_sem.at[2]),
    ]
    for load in loads:
        load.start()
    for f in range(feats):
        table[ring, f, line] = grad_ref[:, f * LANES : (f + 1) * LANES]
    padded = jnp.concatenate(
        [
            score_ref[...].astype(jnp.float32),
            jnp.zeros((tokens, LANES - score_ref.shape[1]), jnp.float32),
        ],
        axis=1,
    )
    table[ring, feats, line] = padded.astype(jnp.bfloat16)
    slot_lane = lax.broadcasted_iota(jnp.int32, (1, cap), 1)
    for e in range(experts):
        ids[0, e : e + 1, :] = jnp.where(
            slot_lane < count_ref[e], routes_ref[e : e + 1, :], -1
        )

    barrier = pltpu.get_barrier_semaphore()
    greeted = [(sibling, chip)]
    greeted += [(node_at(ring, line_peer(d)), chip) for d in range(1, n)]
    greeted += [(node_at(lax.rem(ring + d, n), line), chip) for d in sorted({1, n - 1})]
    greeted += [(node, lax.rem(chip + d, ny)) for d in range(1, ny)]
    for peer in greeted:
        pl.semaphore_signal(
            barrier, inc=1, device_id=peer, device_id_type=pl.DeviceIdType.MESH
        )
    pl.semaphore_wait(barrier, len(greeted))

    def ids_copy():
        return remote(ids.at[0], ids.at[1], ids_send_sem, ids_recv_sem, sibling, chip)

    def line_push(g, d):
        lo, hi = groups[g]
        block = table.at[ring, lo:hi, line]
        return remote(
            block, block, line_send.at[g, d], line_recv.at[g, line], node_at(ring, line_peer(d)), chip
        )

    def line_arrival(g, d):
        lo, hi = groups[g]
        peer = line_peer(d)
        block = table.at[ring, lo:hi, peer]
        return remote(
            block, block, line_send.at[g, d], line_recv.at[g, peer], node_at(ring, peer), chip
        )

    def ring_block(g, way, s, pos):
        lo, hi = groups[g]
        if s < half_ring:
            return table.at[pos, lo:hi]
        return table.at[pos, lo:hi, pl.ds(way * half_ring, half_ring)]

    def ring_copy(g, way, s, arrival):
        step = 1 if way == 0 else n - 1
        hop = s if arrival else s - 1
        pos = lax.rem(ring + (n - step) * hop, n)
        block = ring_block(g, way, s, pos)
        to = node_at(lax.rem(ring + step, n), line)
        return remote(block, block, ring_send.at[g, way, s - 1], ring_recv.at[g, way, s - 1], to, chip)

    def ring_start(g, s):
        for way in range(2):
            ring_copy(g, way, s, False).start()

    def ring_wait(g, s):
        for way in range(2):
            ring_copy(g, way, s, True).wait_recv()

    def chip_copy(f, way, s, arrival):
        step = 1 if way == 0 else ny - 1
        hop = s if arrival else s - 1
        pos = lax.rem(chip + (ny - step) * hop, ny)
        block = picked.at[pos, f] if s < half_chip else picked.at[pos, f, pl.ds(way * (experts // 2), experts // 2)]
        to = lax.rem(chip + step, ny)
        return remote(block, block, chip_send.at[f, way, s - 1], chip_recv.at[f, way, s - 1], node, to)

    def chip_start(f, s):
        for way in range(2):
            chip_copy(f, way, s, False).start()

    def chip_wait(f, s):
        for way in range(2):
            chip_copy(f, way, s, True).wait_recv()

    def pick_copy(f):
        return remote(
            pick_send.at[f], pick_recv.at[f], pick_send_sem.at[f], pick_recv_sem.at[f], sibling, chip
        )

    def build_onehot(side):
        lanes = min(width, LANES)
        for e in range(experts):
            for b in range(cap // LANES):
                row = ids[side, e : e + 1, b * LANES : (b + 1) * LANES]
                col = jnp.transpose(jnp.broadcast_to(row, (LANES, LANES)))[:, :lanes]
                col_node = col >> (TOP_BITS + bits_of(tokens))
                col_core = col_node & 1
                col_z = (col_node >> 1) & (n - 1)
                col_x = col_node >> (1 + nbits)
                col_line = col_x + core * (col_z - col_x)
                col_ring = col_z + core * (col_x - col_z)
                inner = (col >> TOP_BITS) & (tokens - 1)
                key = col_ring * width + col_line * tokens + inner
                key = jnp.where((col >= 0) & (col_core == core), key, -1)
                key = key - lax.broadcasted_iota(jnp.int32, (LANES, lanes), 1)
                first = (side * experts + e) * cap + b * LANES

                def body(p, carry):
                    for h in range(width // lanes):
                        hit = key == p * width + h * lanes
                        onehot[p, first : first + LANES, h * lanes : (h + 1) * lanes] = jnp.where(
                            hit, 1.0, 0.0
                        ).astype(jnp.bfloat16)
                    return carry

                lax.fori_loop(0, n, body, 0)

    def build_low_hot():
        lane = lax.broadcasted_iota(jnp.int32, (LANES, 2 * LANES), 1)
        for e in range(experts):
            for b in range(cap // LANES):
                row = ids[0, e : e + 1, b * LANES : (b + 1) * LANES]
                col = jnp.transpose(jnp.broadcast_to(row, (2 * LANES, LANES)))
                first = e * cap + b * LANES
                low_hot[first : first + LANES, :] = jnp.where(
                    (col & (2 * LANES - 1)) == lane, 1.0, 0.0
                ).astype(jnp.bfloat16)

    def select(lo, hi, side, out):
        def body(e, carry):
            first = pl.multiple_of((side * experts + e) * cap, cap)
            total = jnp.zeros((cap, (hi - lo) * LANES), jnp.float32)
            for p in range(n):
                parts = [table[p, f].reshape(width, LANES) for f in range(lo, hi)]
                rhs = parts[0] if len(parts) == 1 else jnp.concatenate(parts, axis=1)
                total += dot_f32(onehot[p, pl.ds(first, cap), :], rhs)
            for f in range(lo, hi):
                out[f, e] = total[:, (f - lo) * LANES : (f - lo + 1) * LANES].astype(jnp.bfloat16)
            return carry

        lax.fori_loop(0, experts, body, 0)

    def send_picks(lo, hi):
        select(lo, hi, 1, pick_send)
        for f in range(lo, hi):
            pick_copy(f).start()
        select(lo, hi, 0, pick_own)

    def merge(f):
        pick_copy(f).wait_recv()
        picked[chip, f] = pick_own[f] + pick_recv[f]

    def multiply(f, first):
        def body(e, carry):
            total = jnp.zeros((cap, LANES), jnp.float32) if first else back[e]
            for y in range(ny):
                col = (y * feats + f) * LANES
                total += lax.dot_general(
                    picked[y, f, e],
                    w_buf[e, :, col : col + LANES],
                    (((1,), (1,)), ((), ())),
                    preferred_element_type=jnp.float32,
                )
            back[e] = total
            return carry

        lax.fori_loop(0, experts, body, 0)

    ids_copy().start()
    for g in range(2):
        for d in range(1, n):
            line_push(g, d).start()
    build_onehot(0)
    for d in range(1, n):
        line_arrival(0, d).wait_recv()
    ring_start(0, 1)
    ids_copy().wait_recv()
    build_onehot(1)
    for s in range(1, half_ring):
        ring_wait(0, s)
        ring_start(0, s + 1)
    for d in range(1, n):
        line_arrival(1, d).wait_recv()
    ring_start(1, 1)
    ring_wait(0, half_ring)
    send_picks(0, 1)
    build_low_hot()
    merge(0)
    chip_start(0, 1)
    for load in loads:
        load.wait()
    for s in range(1, half_ring):
        ring_wait(1, s)
        ring_start(1, s + 1)
        if s < half_chip:
            chip_wait(0, s)
            chip_start(0, s + 1)
    ring_wait(1, half_ring)
    for lo in range(1, feats, 2):
        send_picks(lo, lo + 2)
        for f in range(lo, min(lo + 2, feats)):
            merge(f)
            chip_start(f, 1)
    for s in range(half_ring, half_chip):
        chip_wait(0, s)
        chip_start(0, s + 1)
    merge_scores = feats
    pick_copy(merge_scores).wait_recv()
    chip_wait(0, half_chip)
    multiply(0, True)
    for s in range(1, half_chip):
        for f in range(1, feats):
            chip_wait(f, s)
            chip_start(f, s + 1)
    for f in range(1, feats):
        chip_wait(f, half_chip)
        multiply(f, False)

    for e in range(experts):
        for b in range(cap // LANES):
            rows = slice(b * LANES, (b + 1) * LANES)
            g = gate_buf[e, rows, :].astype(jnp.float32)
            u = up_buf[e, rows, :].astype(jnp.float32)
            bk = back[e, rows, :]
            s = 1.0 / (1.0 + jnp.exp(-g))
            silu = g * s
            row = ids[0, e : e + 1, b * LANES : (b + 1) * LANES]
            place = jnp.transpose(jnp.broadcast_to(row, (LANES, LANES))) & ((1 << TOP_BITS) - 1)
            lane = lax.broadcasted_iota(jnp.int32, (LANES, LANES), 1)
            scores = pick_own[feats, e, rows, :].astype(jnp.float32) + pick_recv[
                feats, e, rows, :
            ].astype(jnp.float32)
            weight = jnp.sum(jnp.where(place == lane, scores, 0.0), axis=1, keepdims=True)
            product = silu * u * bk
            at = e * (cap // LANES) + b
            sums[chip, at : at + 1, :] = jnp.sum(jnp.transpose(product), axis=0, keepdims=True)
            scaled = weight * bk
            grad_gate_ref[e, rows, :] = (scaled * u * (s * (1.0 + g * (1.0 - s)))).astype(jnp.bfloat16)
            grad_up_ref[e, rows, :] = (scaled * silu).astype(jnp.bfloat16)

    def sum_copy(d, slot):
        return remote(
            sums.at[slot], sums.at[slot], sum_send.at[d], sum_recv.at[slot], node, lax.rem(chip + d, ny)
        )

    for d in range(1, ny):
        sum_copy(d, chip).start()
    for d in range(1, ny):
        sum_copy(d, lax.rem(chip + d, ny)).wait_recv()
    full = sums[0]
    for y in range(1, ny):
        full = full + sums[y]

    targets = 2 * n
    pieces = []
    for e in range(experts):
        for b in range(cap // LANES):
            at = e * (cap // LANES) + b
            row_node = ids[0, e : e + 1, b * LANES : (b + 1) * LANES] >> (TOP_BITS + bits_of(tokens))
            row_z = (row_node >> 1) & (n - 1)
            row_x = row_node >> (1 + nbits)
            row_target = jnp.where(
                ((row_z - row_x) & (n - 1)) == chip, row_x * 2 + (row_node & 1), -1
            )
            target = lax.broadcasted_iota(jnp.int32, (targets, LANES), 0)
            pieces.append(jnp.where(row_target == target, full[at : at + 1, :], 0.0))
    spread = jnp.concatenate(pieces, axis=1)
    high = spread.astype(jnp.bfloat16)
    rest = spread - high.astype(jnp.float32)
    middle = rest.astype(jnp.bfloat16)
    low = (rest - middle.astype(jnp.float32)).astype(jnp.bfloat16)
    dense = dot_f32(high, low_hot[...]) + dot_f32(middle, low_hot[...]) + dot_f32(low, low_hot[...])
    for i in range(targets):
        dense_send[i, 0:1, :] = dense[i : i + 1, :LANES]
        dense_send[i, 1:2, :] = dense[i : i + 1, LANES:]

    def dense_copy(i):
        at_x = i // 2
        at_z = lax.rem(at_x + chip, n)
        to = (at_x * n + at_z) * 2 + lax.rem(i, 2)
        return to, remote(
            dense_send.at[i], dense_recv.at[node], dense_send_sem.at[i], dense_recv_sem, to, chip
        )

    def dense_start(i, carry):
        to, copy = dense_copy(i)

        @pl.when(to != node)
        def _():
            copy.start()

        return carry

    lax.fori_loop(0, targets, dense_start, 0)
    owner = lax.rem(z - x + n, n) == chip

    def total_copy(d):
        return remote(
            total_buf, total_buf, total_send.at[d], total_recv, node, lax.rem(chip + d, ny)
        )

    @pl.when(owner)
    def _():
        dense_recv[node] = dense_send[2 * x + core]
        others = dense_recv.at[pl.ds(0, dense_recv.shape[0] - 1)]
        pltpu.make_async_copy(others, others, dense_recv_sem).wait()
        total_buf[...] = jnp.sum(dense_recv[...], axis=0)
        for d in range(1, ny):
            total_copy(d).start()
        for d in range(1, ny):
            total_copy(d).wait_send()

    @pl.when(jnp.logical_not(owner))
    def _():
        total_copy(1).wait_recv()

    grad_score_ref[...] = total_buf[...]

    def dense_sent(i, carry):
        to, copy = dense_copy(i)

        @pl.when(to != node)
        def _():
            copy.wait_send()

        return carry

    lax.fori_loop(0, targets, dense_sent, 0)
    ids_copy().wait_send()
    for g in range(2):
        for d in range(1, n):
            line_push(g, d).wait_send()
        for s in range(1, half_ring + 1):
            for way in range(2):
                ring_copy(g, way, s, False).wait_send()
    for f in range(chunks):
        pick_copy(f).wait_send()
    for f in range(feats):
        for s in range(1, half_chip + 1):
            for way in range(2):
                chip_copy(f, way, s, False).wait_send()
    for d in range(1, ny):
        sum_copy(d, chip).wait_send()


def on_device(n, ny, grad_out, route_score, expert_routes, expert_count, gate_pre, up_pre, w_down):
    tokens, features = grad_out.shape
    experts, cap = expert_routes.shape
    hidden = gate_pre.shape[2]
    feats = features // LANES
    chunks = feats + 1
    slots = experts * cap
    nodes = 2 * n * n
    targets = 2 * n
    half_ring, half_chip = max(n // 2, 1), max(ny // 2, 1)
    bf16, f32 = jnp.bfloat16, jnp.float32
    dma = pltpu.SemaphoreType.DMA
    vmem = pl.BlockSpec(memory_space=pltpu.VMEM)
    hbm = pl.BlockSpec(memory_space=pl.ANY)
    grad_gate, grad_up, score = pl.pallas_call(
        functools.partial(kernel, n, ny),
        out_shape=(
            jax.ShapeDtypeStruct(gate_pre.shape, bf16),
            jax.ShapeDtypeStruct(gate_pre.shape, bf16),
            jax.ShapeDtypeStruct((2, LANES), f32),
        ),
        in_specs=[vmem, vmem, vmem, pl.BlockSpec(memory_space=pltpu.SMEM), hbm, hbm, hbm],
        out_specs=(vmem, vmem, vmem),
        scratch_shapes=[
            pltpu.VMEM((n, chunks, n, tokens, LANES), bf16),
            pltpu.VMEM((n, 2 * slots, n * tokens), bf16),
            pltpu.VMEM((2, experts, cap), jnp.int32),
            pltpu.VMEM((chunks, experts, cap, LANES), bf16),
            pltpu.VMEM((chunks, experts, cap, LANES), bf16),
            pltpu.VMEM((chunks, experts, cap, LANES), bf16),
            pltpu.VMEM((ny, feats, experts, cap, LANES), bf16),
            pltpu.VMEM(gate_pre.shape, bf16),
            pltpu.VMEM(up_pre.shape, bf16),
            pltpu.VMEM(w_down.shape, bf16),
            pltpu.VMEM((experts, cap, hidden), f32),
            pltpu.VMEM((slots, 2 * LANES), bf16),
            pltpu.VMEM((ny, slots // LANES, LANES), f32),
            pltpu.VMEM((targets, 2, LANES), f32),
            pltpu.VMEM((nodes, 2, LANES), f32),
            pltpu.VMEM((2, LANES), f32),
            dma((3,)),
            dma,
            dma,
            dma((2, n)),
            dma((2, n)),
            dma((2, 2, half_ring)),
            dma((2, 2, half_ring)),
            dma((chunks,)),
            dma((chunks,)),
            dma((feats, 2, half_chip)),
            dma((feats, 2, half_chip)),
            dma((ny,)),
            dma((ny,)),
            dma((targets,)),
            dma,
            dma((ny,)),
            dma,
        ],
        compiler_params=pltpu.CompilerParams(
            collective_id=0, has_side_effects=True, vmem_limit_bytes=40 * 1024 * 1024
        ),
        name="expert_backward",
    )(grad_out, route_score, expert_routes, expert_count, gate_pre, up_pre, w_down)
    return grad_gate, grad_up, score.reshape(tokens, -1)


def solution(mesh):
    ny = mesh.shape["chip"]
    n = 1
    while 2 * n * n < mesh.shape["node"]:
        n *= 2
    placed = (
        P("node", "chip"),
        P("node", None),
        P("node", None),
        P("node"),
        P("node", None, "chip"),
        P("node", None, "chip"),
        P("node", "chip", None),
    )
    return jax.shard_map(
        functools.partial(on_device, n, ny),
        mesh=mesh,
        in_specs=placed,
        out_specs=(P("node", None, "chip"), P("node", None, "chip"), P("node", None)),
        check_vma=False,
    )
```

```python
import functools

import jax
import jax.numpy as jnp
from jax import lax
from jax.experimental import pallas as pl
from jax.experimental.pallas import tpu as pltpu
from jax.sharding import PartitionSpec as P

LANES = 128
TOP_BITS = 3


def bits_of(size):
    return size.bit_length() - 1


def dot_f32(a, b):
    return jnp.dot(a, b, preferred_element_type=jnp.float32)


def remote(src, dst, send, recv, node, chip):
    return pltpu.make_async_remote_copy(
        src_ref=src,
        dst_ref=dst,
        send_sem=send,
        recv_sem=recv,
        device_id=(node, chip),
        device_id_type=pl.DeviceIdType.MESH,
    )


def kernel(
    n,
    ny,
    grad_hbm,
    score_ref,
    routes_hbm,
    count_hbm,
    gate_hbm,
    up_hbm,
    w_hbm,
    grad_gate_ref,
    grad_up_ref,
    grad_score_ref,
    grad_ref,
    routes_ref,
    count_ref,
    table,
    onehot,
    ids,
    pick_send,
    pick_recv,
    pick_own,
    picked,
    gate_buf,
    up_buf,
    w_buf,
    back,
    low_hot,
    sums,
    dense_send,
    dense_recv,
    totals,
    in_sem,
    ids_send_sem,
    ids_recv_sem,
    line_send,
    line_recv,
    slab_send,
    slab_recv,
    wide_send,
    wide_recv,
    ring_send,
    ring_recv,
    pick_send_sem,
    pick_recv_sem,
    chip_send,
    chip_recv,
    sum_send,
    sum_recv,
    dense_send_sem,
    dense_recv_sem,
    total_send,
    total_recv,
):
    units = table.shape[1]
    tokens = table.shape[3]
    experts, cap = routes_ref.shape
    slots = experts * cap
    width = n * tokens
    half_ring, half_chip = n // 2, ny // 2
    nbits = bits_of(n)
    feats = w_buf.shape[2] // (ny * LANES)
    rounds = feats - 1
    scores, slices = rounds, rounds + 1
    apart = [0]
    for d in range(1, half_chip):
        apart += [d, -d]
    apart += [half_chip]
    pushes = ((0, 1), (1, slices + 1))
    rings = [(1, rounds), (scores, slices + 1)]
    for lo in range(slices + 1, max(units - 1, slices + 2), 2):
        rings.append((lo, units if lo + 3 >= units else lo + 2))

    node = lax.axis_index("node")
    chip = lax.axis_index("chip")
    core = lax.rem(node, 2)
    z = lax.rem(node // 2, n)
    x = node // (2 * n)
    line = x + core * (z - x)
    ring = z + core * (x - z)
    sibling = node + 1 - 2 * core

    def node_at(ring_pos, line_pos):
        at_x = line_pos + core * (ring_pos - line_pos)
        at_z = ring_pos + core * (line_pos - ring_pos)
        return (at_x * n + at_z) * 2 + core

    def line_peer(d):
        return lax.rem(line + d, n)

    loads = [
        pltpu.make_async_copy(src, dst, in_sem.at[i])
        for i, (src, dst) in enumerate(
            (
                (grad_hbm, grad_ref),
                (routes_hbm, routes_ref),
                (count_hbm, count_ref),
                (w_hbm, w_buf),
                (gate_hbm, gate_buf),
                (up_hbm, up_buf),
            )
        )
    ]
    for load in loads:
        load.start()

    barrier = pltpu.get_barrier_semaphore()
    greeted = [(sibling, chip)]
    greeted += [(node_at(ring, line_peer(d)), chip) for d in range(1, n)]
    greeted += [(node_at(lax.rem(ring + d, n), line), chip) for d in range(1, n)]
    greeted += [(node, lax.rem(chip + d, ny)) for d in range(1, ny)]
    for peer in greeted:
        pl.semaphore_signal(
            barrier, inc=1, device_id=peer, device_id_type=pl.DeviceIdType.MESH
        )

    for load in loads[:3]:
        load.wait()
    for f in range(rounds):
        table[ring, f, line] = grad_ref[:, f * LANES : (f + 1) * LANES]
    table[ring, slices, line] = grad_ref[:, rounds * LANES : feats * LANES]
    tops = score_ref.shape[0]
    padded = jnp.concatenate(
        [score_ref[...].astype(jnp.float32), jnp.zeros((tops, LANES - tokens), jnp.float32)], axis=1
    )
    padded = jnp.concatenate([padded, jnp.zeros((LANES - tops, LANES), jnp.float32)], axis=0)
    table[ring, scores, line] = jnp.transpose(padded)[:tokens].astype(jnp.bfloat16)
    slot_lane = lax.broadcasted_iota(jnp.int32, (1, cap), 1)
    for e in range(experts):
        ids[0, e : e + 1, :] = jnp.where(
            slot_lane < count_ref[e], routes_ref[e : e + 1, :], -1
        )
    pl.semaphore_wait(barrier, len(greeted))

    def ids_copy():
        return remote(ids.at[0], ids.at[1], ids_send_sem, ids_recv_sem, sibling, chip)

    far_first = sorted(range(1, n), key=lambda d: -min(d, n - d))

    def line_push(g, d):
        lo, hi = pushes[g]
        block = table.at[ring, lo:hi, line]
        return remote(
            block, block, line_send.at[g, d], line_recv.at[g, line], node_at(ring, line_peer(d)), chip
        )

    def line_start(g):
        for d in far_first:
            line_push(g, d).start()

    def line_wait(g):
        lo, hi = pushes[g]
        for d in range(1, n):
            peer = line_peer(d)
            block = table.at[ring, lo:hi, peer]
            remote(
                block, block, line_send.at[g, d], line_recv.at[g, peer], node_at(ring, peer), chip
            ).wait_recv()

    def apart_chip(i):
        return lax.rem(chip + apart[i] + ny, ny)

    def slab_copy(i, arrival):
        back_i = i if apart[i] == half_chip else apart.index(-apart[i])
        mine = table.at[ring, slices]
        if arrival:
            block = table.at[ring, slices + i]
            return remote(block, block, slab_send.at[i], slab_recv.at[i], node, apart_chip(i))
        there = table.at[ring, slices + back_i]
        return remote(mine, there, slab_send.at[i], slab_recv.at[back_i], node, apart_chip(i))

    def slab_wait(*which):
        for i in which:
            if i < ny:
                slab_copy(i, True).wait_recv()

    def wide_push(d):
        block = table.at[ring, 0]
        peer = lax.rem(ring + d, n)
        return remote(
            block, block, wide_send.at[d], wide_recv.at[ring], node_at(peer, line), chip
        )

    def wide_wait():
        for d in range(1, n):
            peer = lax.rem(ring + d, n)
            block = table.at[peer, 0]
            remote(
                block, block, wide_send.at[d], wide_recv.at[peer], node_at(peer, line), chip
            ).wait_recv()

    def ring_block(g, way, s, pos):
        lo, hi = rings[g]
        if s < half_ring:
            return table.at[pos, lo:hi]
        return table.at[pos, lo:hi, pl.ds(way * half_ring, half_ring)]

    def ring_copy(g, way, s, arrival):
        step = 1 if way == 0 else n - 1
        hop = s if arrival else s - 1
        pos = lax.rem(ring + (n - step) * hop, n)
        block = ring_block(g, way, s, pos)
        to = node_at(lax.rem(ring + step, n), line)
        return remote(block, block, ring_send.at[g, way, s - 1], ring_recv.at[g, way, s - 1], to, chip)

    def ring_start(g, s):
        if g < len(rings):
            for way in range(2):
                ring_copy(g, way, s, False).start()

    def ring_go(g, s):
        if g < len(rings) and s <= half_ring:
            for way in range(2):
                ring_copy(g, way, s, True).wait_recv()
            if s < half_ring:
                ring_start(g, s + 1)

    def chip_copy(f, way, s, arrival):
        step = 1 if way == 0 else ny - 1
        hop = s if arrival else s - 1
        pos = lax.rem(chip + (ny - step) * hop, ny)
        block = picked.at[pos, f] if s < half_chip else picked.at[pos, f, pl.ds(way * (experts // 2), experts // 2)]
        to = lax.rem(chip + step, ny)
        return remote(block, block, chip_send.at[f, way, s - 1], chip_recv.at[f, way, s - 1], node, to)

    def chip_start(f, s):
        for way in range(2):
            chip_copy(f, way, s, False).start()

    def chip_go(f, s):
        if s <= half_chip:
            for way in range(2):
                chip_copy(f, way, s, True).wait_recv()
            if s < half_chip:
                chip_start(f, s + 1)

    def pick_copy(f):
        return remote(
            pick_send.at[f], pick_recv.at[f], pick_send_sem.at[f], pick_recv_sem.at[f], sibling, chip
        )

    def build_onehot(side):
        lanes = min(width, LANES)
        for e in range(experts):
            for b in range(cap // LANES):
                row = ids[side, e : e + 1, b * LANES : (b + 1) * LANES]
                col = jnp.transpose(jnp.broadcast_to(row, (LANES, LANES)))[:, :lanes]
                col_node = col >> (TOP_BITS + bits_of(tokens))
                col_core = col_node & 1
                col_z = (col_node >> 1) & (n - 1)
                col_x = col_node >> (1 + nbits)
                col_line = col_x + core * (col_z - col_x)
                col_ring = col_z + core * (col_x - col_z)
                inner = (col >> TOP_BITS) & (tokens - 1)
                key = col_ring * width + col_line * tokens + inner
                key = jnp.where((col >= 0) & (col_core == core), key, -1)
                key = key - lax.broadcasted_iota(jnp.int32, (LANES, lanes), 1)
                first = (side * experts + e) * cap + b * LANES

                def body(p, carry):
                    for h in range(width // lanes):
                        hit = key == p * width + h * lanes
                        onehot[p, first : first + LANES, h * lanes : (h + 1) * lanes] = jnp.where(
                            hit, 1.0, 0.0
                        ).astype(jnp.bfloat16)
                    return carry

                lax.fori_loop(0, n, body, 0)

    def build_low_hot():
        lane = lax.broadcasted_iota(jnp.int32, (LANES, 2 * LANES), 1)
        for e in range(experts):
            for b in range(cap // LANES):
                row = ids[0, e : e + 1, b * LANES : (b + 1) * LANES]
                col = jnp.transpose(jnp.broadcast_to(row, (2 * LANES, LANES)))
                first = e * cap + b * LANES
                low_hot[first : first + LANES, :] = jnp.where(
                    (col & (2 * LANES - 1)) == lane, 1.0, 0.0
                ).astype(jnp.bfloat16)

    def select(lo, hi, side, out):
        def body(e, carry):
            first = pl.multiple_of((side * experts + e) * cap, cap)
            total = jnp.zeros((cap, (hi - lo) * LANES), jnp.float32)
            for p in range(n):
                parts = [table[p, f].reshape(width, LANES) for f in range(lo, hi)]
                rhs = parts[0] if len(parts) == 1 else jnp.concatenate(parts, axis=1)
                total += dot_f32(onehot[p, pl.ds(first, cap), :], rhs)
            for f in range(lo, hi):
                out[f, e] = total[:, (f - lo) * LANES : (f - lo + 1) * LANES].astype(jnp.bfloat16)
            return carry

        lax.fori_loop(0, experts, body, 0)

    def send_picks(lo, hi):
        select(lo, hi, 1, pick_send)
        for f in range(lo, hi):
            pick_copy(f).start()
        select(lo, hi, 0, pick_own)

    def merge(unit, owner, f):
        pick_copy(unit).wait_recv()
        picked[owner, f] = pick_own[unit] + pick_recv[unit]

    def multiply(f, first):
        def body(e, carry):
            total = jnp.zeros((cap, LANES), jnp.float32) if first else back[e]
            for y in range(ny):
                col = (y * feats + f) * LANES
                total += lax.dot_general(
                    picked[y, f, e],
                    w_buf[e, :, col : col + LANES],
                    (((1,), (1,)), ((), ())),
                    preferred_element_type=jnp.float32,
                )
            back[e] = total
            return carry

        lax.fori_loop(0, experts, body, 0)

    def ring_picks(g):
        if g < len(rings):
            lo, hi = rings[g]
            for first in range(lo, hi, 2):
                send_picks(first, min(first + 2, hi))

    line_start(0)
    ids_copy().start()
    line_start(1)
    build_onehot(0)
    line_wait(0)
    for d in far_first:
        wide_push(d).start()
    ids_copy().wait_recv()
    build_onehot(1)
    line_wait(1)
    ring_start(0, 1)
    for i in range(1, ny):
        slab_copy(i, False).start()
    ring_start(1, 1)
    build_low_hot()
    ring_go(0, 1)
    slab_wait(1, 2)
    ring_start(2, 1)
    wide_wait()
    send_picks(0, 1)
    ring_go(1, 1)
    ring_go(0, 2)
    slab_wait(3, 4)
    ring_start(3, 1)
    merge(0, chip, 0)
    chip_start(0, 1)
    ring_go(2, 1)
    ring_go(1, 2)
    slab_wait(5, 6, 7)
    ring_start(4, 1)
    ring_go(0, 3)
    chip_go(0, 1)
    ring_go(3, 1)
    ring_go(2, 2)
    ring_go(1, 3)
    ring_go(0, 4)
    ring_picks(0)
    chip_go(0, 2)
    for f in range(1, rounds):
        merge(f, chip, f)
        chip_start(f, 1)
    ring_go(4, 1)
    ring_go(3, 2)
    ring_go(2, 3)
    ring_go(1, 4)
    ring_picks(1)
    chip_go(0, 3)
    for load in loads[3:]:
        load.wait()
    ring_go(4, 2)
    ring_go(3, 3)
    ring_go(2, 4)
    chip_go(1, 1)
    chip_go(2, 1)
    ring_picks(2)
    chip_go(0, 4)
    ring_go(4, 3)
    ring_go(3, 4)
    chip_go(1, 2)
    chip_go(2, 2)
    ring_picks(3)
    multiply(0, True)
    ring_go(4, 4)
    chip_go(1, 3)
    chip_go(2, 3)
    ring_picks(4)
    for i in range(ny):
        merge(slices + i, apart_chip(i), rounds)
    multiply(rounds, False)
    pick_copy(scores).wait_recv()
    chip_go(1, 4)
    multiply(1, False)
    chip_go(2, 4)
    multiply(2, False)

    for e in range(experts):
        for b in range(cap // LANES):
            rows = slice(b * LANES, (b + 1) * LANES)
            g = gate_buf[e, rows, :].astype(jnp.float32)
            u = up_buf[e, rows, :].astype(jnp.float32)
            bk = back[e, rows, :]
            s = 1.0 / (1.0 + jnp.exp(-g))
            silu = g * s
            row = ids[0, e : e + 1, b * LANES : (b + 1) * LANES]
            place = jnp.transpose(jnp.broadcast_to(row, (LANES, LANES))) & ((1 << TOP_BITS) - 1)
            lane = lax.broadcasted_iota(jnp.int32, (LANES, LANES), 1)
            spread = pick_own[scores, e, rows, :].astype(jnp.float32) + pick_recv[
                scores, e, rows, :
            ].astype(jnp.float32)
            weight = jnp.sum(jnp.where(place == lane, spread, 0.0), axis=1, keepdims=True)
            product = silu * u * bk
            at = e * (cap // LANES) + b
            sums[chip, at : at + 1, :] = jnp.sum(jnp.transpose(product), axis=0, keepdims=True)
            scaled = weight * bk
            grad_gate_ref[e, rows, :] = (scaled * u * (s * (1.0 + g * (1.0 - s)))).astype(jnp.bfloat16)
            grad_up_ref[e, rows, :] = (scaled * silu).astype(jnp.bfloat16)

    def sum_copy(d, slot):
        return remote(
            sums.at[slot], sums.at[slot], sum_send.at[d], sum_recv.at[slot], node, lax.rem(chip + d, ny)
        )

    for d in range(1, ny):
        sum_copy(d, chip).start()
    for d in range(1, ny):
        sum_copy(d, lax.rem(chip + d, ny)).wait_recv()
    full = sums[0]
    for y in range(1, ny):
        full = full + sums[y]

    targets = 2 * n
    pieces = []
    for e in range(experts):
        for b in range(cap // LANES):
            at = e * (cap // LANES) + b
            row_node = ids[0, e : e + 1, b * LANES : (b + 1) * LANES] >> (TOP_BITS + bits_of(tokens))
            row_z = (row_node >> 1) & (n - 1)
            row_x = row_node >> (1 + nbits)
            row_target = jnp.where(
                ((row_z - z) & (n - 1)) == chip, row_x * 2 + (row_node & 1), -1
            )
            target = lax.broadcasted_iota(jnp.int32, (targets, LANES), 0)
            pieces.append(jnp.where(row_target == target, full[at : at + 1, :], 0.0))
    spread = jnp.concatenate(pieces, axis=1)
    high = spread.astype(jnp.bfloat16)
    rest = spread - high.astype(jnp.float32)
    middle = rest.astype(jnp.bfloat16)
    low = (rest - middle.astype(jnp.float32)).astype(jnp.bfloat16)
    dense = dot_f32(high, low_hot[...]) + dot_f32(middle, low_hot[...]) + dot_f32(low, low_hot[...])
    for i in range(targets):
        dense_send[i, 0:1, :] = dense[i : i + 1, :LANES]
        dense_send[i, 1:2, :] = dense[i : i + 1, LANES:]

    mine = 2 * x + core

    def dense_node(i, shift):
        return ((i // 2) * n + lax.rem(z + shift, n)) * 2 + lax.rem(i, 2)

    def dense_copy(i, slot, to):
        return remote(
            dense_send.at[i], dense_recv.at[slot], dense_send_sem.at[i], dense_recv_sem.at[slot], to, chip
        )

    def each_target(act, shift):
        def body(i, carry):
            to = dense_node(i, shift)

            @pl.when(to != node)
            def _():
                act(i, to)

            return carry

        lax.fori_loop(0, targets, body, 0)

    each_target(lambda i, to: dense_copy(i, mine, to).start(), chip)

    @pl.when(chip == 0)
    def _():
        dense_recv[mine] = dense_send[mine]

    each_target(lambda i, to: dense_copy(i, i, to).wait_recv(), n - chip)
    totals[chip] = jnp.sum(dense_recv[...], axis=0)

    def total_copy(d, slot):
        return remote(
            totals.at[slot], totals.at[slot], total_send.at[d], total_recv.at[slot], node, lax.rem(chip + d, ny)
        )

    for d in range(1, ny):
        total_copy(d, chip).start()
    for d in range(1, ny):
        total_copy(d, lax.rem(chip + d, ny)).wait_recv()
    grad_score_ref[...] = jnp.sum(totals[...], axis=0)

    each_target(lambda i, to: dense_copy(i, mine, to).wait_send(), chip)
    ids_copy().wait_send()
    for d in range(1, n):
        wide_push(d).wait_send()
        for g in range(2):
            line_push(g, d).wait_send()
    for g in range(len(rings)):
        for s in range(1, half_ring + 1):
            for way in range(2):
                ring_copy(g, way, s, False).wait_send()
    for u in range(units):
        pick_copy(u).wait_send()
    for f in range(rounds):
        for s in range(1, half_chip + 1):
            for way in range(2):
                chip_copy(f, way, s, False).wait_send()
    for d in range(1, ny):
        slab_copy(d, False).wait_send()
        sum_copy(d, chip).wait_send()
        total_copy(d, chip).wait_send()


def on_device(n, ny, grad_out, route_score, expert_routes, expert_count, gate_pre, up_pre, w_down):
    tokens, features = grad_out.shape
    experts, cap = expert_routes.shape
    hidden = gate_pre.shape[2]
    feats = features // LANES
    units = feats + ny
    slots = experts * cap
    targets = 2 * n
    half_ring, half_chip = max(n // 2, 1), max(ny // 2, 1)
    bf16, f32 = jnp.bfloat16, jnp.float32
    dma = pltpu.SemaphoreType.DMA
    vmem = pl.BlockSpec(memory_space=pltpu.VMEM)
    hbm = pl.BlockSpec(memory_space=pltpu.HBM)
    grad_gate, grad_up, score = pl.pallas_call(
        functools.partial(kernel, n, ny),
        out_shape=(
            jax.ShapeDtypeStruct(gate_pre.shape, bf16),
            jax.ShapeDtypeStruct(gate_pre.shape, bf16),
            jax.ShapeDtypeStruct((2, LANES), f32),
        ),
        in_specs=[hbm, vmem, hbm, hbm, hbm, hbm, hbm],
        out_specs=(vmem, vmem, vmem),
        scratch_shapes=[
            pltpu.VMEM(grad_out.shape, bf16),
            pltpu.VMEM(expert_routes.shape, jnp.int32),
            pltpu.SMEM(expert_count.shape, jnp.int32),
            pltpu.VMEM((n, units, n, tokens, LANES), bf16),
            pltpu.VMEM((n, 2 * slots, n * tokens), bf16),
            pltpu.VMEM((2, experts, cap), jnp.int32),
            pltpu.VMEM((units, experts, cap, LANES), bf16),
            pltpu.VMEM((units, experts, cap, LANES), bf16),
            pltpu.VMEM((units, experts, cap, LANES), bf16),
            pltpu.VMEM((ny, feats, experts, cap, LANES), bf16),
            pltpu.VMEM(gate_pre.shape, bf16),
            pltpu.VMEM(up_pre.shape, bf16),
            pltpu.VMEM(w_down.shape, bf16),
            pltpu.VMEM((experts, cap, hidden), f32),
            pltpu.VMEM((slots, 2 * LANES), bf16),
            pltpu.VMEM((ny, slots // LANES, LANES), f32),
            pltpu.VMEM((targets, 2, LANES), f32),
            pltpu.VMEM((targets, 2, LANES), f32),
            pltpu.VMEM((ny, 2, LANES), f32),
            dma((6,)),
            dma,
            dma,
            dma((2, n)),
            dma((2, n)),
            dma((ny,)),
            dma((ny,)),
            dma((n,)),
            dma((n,)),
            dma((units // 2, 2, half_ring)),
            dma((units // 2, 2, half_ring)),
            dma((units,)),
            dma((units,)),
            dma((feats - 1, 2, half_chip)),
            dma((feats - 1, 2, half_chip)),
            dma((ny,)),
            dma((ny,)),
            dma((targets,)),
            dma((targets,)),
            dma((ny,)),
            dma((ny,)),
        ],
        compiler_params=pltpu.CompilerParams(
            collective_id=0, has_side_effects=True, vmem_limit_bytes=63 * 1024 * 1024
        ),
        name="expert_backward",
    )(grad_out, route_score.T, expert_routes, expert_count, gate_pre, up_pre, w_down)
    return grad_gate, grad_up, score.reshape(tokens, -1)


def solution(mesh):
    ny = mesh.shape["chip"]
    n = 1
    while 2 * n * n < mesh.shape["node"]:
        n *= 2
    placed = (
        P("node", "chip"),
        P("node", None),
        P("node", None),
        P("node"),
        P("node", None, "chip"),
        P("node", None, "chip"),
        P("node", "chip", None),
    )
    return jax.shard_map(
        functools.partial(on_device, n, ny),
        mesh=mesh,
        in_specs=placed,
        out_specs=(P("node", None, "chip"), P("node", None, "chip"), P("node", None)),
        check_vma=False,
    )
```

```python
import functools

import jax
import jax.numpy as jnp
from jax import lax
from jax.experimental import pallas as pl
from jax.experimental.pallas import tpu as pltpu
from jax.sharding import PartitionSpec as P

LANES = 128
TOP_BITS = 3
NEAR = 1


def bits_of(size):
    return size.bit_length() - 1


def dot_f32(a, b):
    return jnp.dot(a, b, preferred_element_type=jnp.float32)


def near_steps(ny):
    return max(min(NEAR, ny // 2 - 1), 0)


def far_chips(ny):
    apart = [0]
    for d in range(near_steps(ny) + 1, ny // 2):
        apart += [d, -d]
    return apart + [ny // 2]


def remote(src, dst, send, recv, node, chip):
    return pltpu.make_async_remote_copy(
        src_ref=src,
        dst_ref=dst,
        send_sem=send,
        recv_sem=recv,
        device_id=(node, chip),
        device_id_type=pl.DeviceIdType.MESH,
    )


def kernel(
    n,
    ny,
    grad_hbm,
    score_ref,
    routes_hbm,
    count_hbm,
    gate_hbm,
    up_hbm,
    w_hbm,
    grad_gate_ref,
    grad_up_ref,
    grad_score_ref,
    grad_ref,
    routes_ref,
    count_ref,
    table,
    onehot,
    ids,
    pick_send,
    pick_recv,
    pick_own,
    picked,
    gate_buf,
    up_buf,
    w_buf,
    back,
    low_hot,
    sums,
    dense_send,
    dense_recv,
    totals,
    in_sem,
    ids_send_sem,
    ids_recv_sem,
    line_send,
    line_recv,
    slab_send,
    slab_recv,
    wide_send,
    wide_recv,
    ring_send,
    ring_recv,
    pick_send_sem,
    pick_recv_sem,
    chip_send,
    chip_recv,
    sum_send,
    sum_recv,
    dense_send_sem,
    dense_recv_sem,
    total_send,
    total_recv,
):
    units = table.shape[1]
    tokens = table.shape[3]
    experts, cap = routes_ref.shape
    slots = experts * cap
    width = n * tokens
    half_ring, half_chip = n // 2, ny // 2
    nbits = bits_of(n)
    feats = w_buf.shape[2] // (ny * LANES)
    rounds = feats - 1
    scores, slices = rounds, rounds + 1
    reach = near_steps(ny)
    apart = far_chips(ny)
    pushes = ((0, 1), (1, slices + 1))
    rings = [(scores, slices + 1)]
    for lo in range(slices + 1, max(units - 1, slices + 2), 2):
        rings.append((lo, units if lo + 3 >= units else lo + 2))

    def last_step(f):
        return reach if f == rounds else half_chip

    node = lax.axis_index("node")
    chip = lax.axis_index("chip")
    core = lax.rem(node, 2)
    z = lax.rem(node // 2, n)
    x = node // (2 * n)
    line = x + core * (z - x)
    ring = z + core * (x - z)
    sibling = node + 1 - 2 * core

    def node_at(ring_pos, line_pos):
        at_x = line_pos + core * (ring_pos - line_pos)
        at_z = ring_pos + core * (line_pos - ring_pos)
        return (at_x * n + at_z) * 2 + core

    def line_peer(d):
        return lax.rem(line + d, n)

    loads = [
        pltpu.make_async_copy(src, dst, in_sem.at[i])
        for i, (src, dst) in enumerate(
            (
                (grad_hbm, grad_ref),
                (routes_hbm, routes_ref),
                (count_hbm, count_ref),
                (w_hbm, w_buf),
                (gate_hbm, gate_buf),
                (up_hbm, up_buf),
            )
        )
    ]
    for load in loads:
        load.start()

    barrier = pltpu.get_barrier_semaphore()
    greeted = [(sibling, chip)]
    greeted += [(node_at(ring, line_peer(d)), chip) for d in range(1, n)]
    greeted += [(node_at(lax.rem(ring + d, n), line), chip) for d in range(1, n)]
    greeted += [(node, lax.rem(chip + d, ny)) for d in range(1, ny)]
    for peer in greeted:
        pl.semaphore_signal(
            barrier, inc=1, device_id=peer, device_id_type=pl.DeviceIdType.MESH
        )

    for load in loads[:3]:
        load.wait()
    for f in range(rounds):
        table[ring, f, line] = grad_ref[:, f * LANES : (f + 1) * LANES]
    table[ring, slices, line] = grad_ref[:, rounds * LANES : feats * LANES]
    tops = score_ref.shape[0]
    padded = jnp.concatenate(
        [score_ref[...].astype(jnp.float32), jnp.zeros((tops, LANES - tokens), jnp.float32)], axis=1
    )
    padded = jnp.concatenate([padded, jnp.zeros((LANES - tops, LANES), jnp.float32)], axis=0)
    table[ring, scores, line] = jnp.transpose(padded)[:tokens].astype(jnp.bfloat16)
    slot_lane = lax.broadcasted_iota(jnp.int32, (1, cap), 1)
    for e in range(experts):
        ids[0, e : e + 1, :] = jnp.where(
            slot_lane < count_ref[e], routes_ref[e : e + 1, :], -1
        )
    pl.semaphore_wait(barrier, len(greeted))

    def ids_copy():
        return remote(ids.at[0], ids.at[1], ids_send_sem, ids_recv_sem, sibling, chip)

    far_first = sorted(range(1, n), key=lambda d: -min(d, n - d))

    def line_push(g, d):
        lo, hi = pushes[g]
        block = table.at[ring, lo:hi, line]
        return remote(
            block, block, line_send.at[g, d], line_recv.at[g, line], node_at(ring, line_peer(d)), chip
        )

    def line_start(g):
        for d in far_first:
            line_push(g, d).start()

    def line_wait(g):
        lo, hi = pushes[g]
        for d in range(1, n):
            peer = line_peer(d)
            block = table.at[ring, lo:hi, peer]
            remote(
                block, block, line_send.at[g, d], line_recv.at[g, peer], node_at(ring, peer), chip
            ).wait_recv()

    def apart_chip(i):
        return lax.rem(chip + apart[i] + ny, ny)

    def slab_copy(i, arrival):
        back_i = i if apart[i] == half_chip else apart.index(-apart[i])
        mine = table.at[ring, slices]
        if arrival:
            block = table.at[ring, slices + i]
            return remote(block, block, slab_send.at[i], slab_recv.at[i], node, apart_chip(i))
        there = table.at[ring, slices + back_i]
        return remote(mine, there, slab_send.at[i], slab_recv.at[back_i], node, apart_chip(i))

    def slab_start():
        for i in range(1, len(apart)):
            slab_copy(i, False).start()

    def slab_wait(*which):
        for i in which:
            if i < len(apart):
                slab_copy(i, True).wait_recv()

    def wide_push(f, d):
        block = table.at[ring, f]
        peer = lax.rem(ring + d, n)
        return remote(
            block, block, wide_send.at[f, d], wide_recv.at[f, ring], node_at(peer, line), chip
        )

    def wide_start(f):
        for d in far_first:
            wide_push(f, d).start()

    def wide_wait(f):
        for d in range(1, n):
            peer = lax.rem(ring + d, n)
            block = table.at[peer, f]
            remote(
                block, block, wide_send.at[f, d], wide_recv.at[f, peer], node_at(peer, line), chip
            ).wait_recv()

    def ring_block(g, way, s, pos):
        lo, hi = rings[g]
        if s < half_ring:
            return table.at[pos, lo:hi]
        return table.at[pos, lo:hi, pl.ds(way * half_ring, half_ring)]

    def ring_copy(g, way, s, arrival):
        step = 1 if way == 0 else n - 1
        hop = s if arrival else s - 1
        pos = lax.rem(ring + (n - step) * hop, n)
        block = ring_block(g, way, s, pos)
        to = node_at(lax.rem(ring + step, n), line)
        return remote(block, block, ring_send.at[g, way, s - 1], ring_recv.at[g, way, s - 1], to, chip)

    def ring_start(g, s):
        if g < len(rings):
            for way in range(2):
                ring_copy(g, way, s, False).start()

    def ring_go(g, s):
        if g < len(rings) and s <= half_ring:
            for way in range(2):
                ring_copy(g, way, s, True).wait_recv()
            if s < half_ring:
                ring_start(g, s + 1)

    def chip_copy(f, way, s, arrival):
        step = 1 if way == 0 else ny - 1
        hop = s if arrival else s - 1
        pos = lax.rem(chip + (ny - step) * hop, ny)
        block = picked.at[pos, f] if s < half_chip else picked.at[pos, f, pl.ds(way * (experts // 2), experts // 2)]
        to = lax.rem(chip + step, ny)
        return remote(block, block, chip_send.at[f, way, s - 1], chip_recv.at[f, way, s - 1], node, to)

    def chip_start(f, s):
        if s <= last_step(f):
            for way in range(2):
                chip_copy(f, way, s, False).start()

    def chip_go(f, s):
        if s <= last_step(f):
            for way in range(2):
                chip_copy(f, way, s, True).wait_recv()
            chip_start(f, s + 1)

    def pick_copy(f):
        return remote(
            pick_send.at[f], pick_recv.at[f], pick_send_sem.at[f], pick_recv_sem.at[f], sibling, chip
        )

    def build_onehot(side):
        lanes = min(width, LANES)
        for e in range(experts):
            for b in range(cap // LANES):
                row = ids[side, e : e + 1, b * LANES : (b + 1) * LANES]
                col = jnp.transpose(jnp.broadcast_to(row, (LANES, LANES)))[:, :lanes]
                col_node = col >> (TOP_BITS + bits_of(tokens))
                col_core = col_node & 1
                col_z = (col_node >> 1) & (n - 1)
                col_x = col_node >> (1 + nbits)
                col_line = col_x + core * (col_z - col_x)
                col_ring = col_z + core * (col_x - col_z)
                inner = (col >> TOP_BITS) & (tokens - 1)
                key = col_ring * width + col_line * tokens + inner
                key = jnp.where((col >= 0) & (col_core == core), key, -1)
                key = key - lax.broadcasted_iota(jnp.int32, (LANES, lanes), 1)
                first = (side * experts + e) * cap + b * LANES

                def body(p, carry):
                    for h in range(width // lanes):
                        hit = key == p * width + h * lanes
                        onehot[p, first : first + LANES, h * lanes : (h + 1) * lanes] = jnp.where(
                            hit, 1.0, 0.0
                        ).astype(jnp.bfloat16)
                    return carry

                lax.fori_loop(0, n, body, 0)

    def build_low_hot():
        lane = lax.broadcasted_iota(jnp.int32, (LANES, 2 * LANES), 1)
        for e in range(experts):
            for b in range(cap // LANES):
                row = ids[0, e : e + 1, b * LANES : (b + 1) * LANES]
                col = jnp.transpose(jnp.broadcast_to(row, (2 * LANES, LANES)))
                first = e * cap + b * LANES
                low_hot[first : first + LANES, :] = jnp.where(
                    (col & (2 * LANES - 1)) == lane, 1.0, 0.0
                ).astype(jnp.bfloat16)

    def select(lo, hi, side, out):
        hi = min(hi, units)
        if lo >= hi:
            return

        def body(e, carry):
            first = pl.multiple_of((side * experts + e) * cap, cap)
            total = jnp.zeros((cap, (hi - lo) * LANES), jnp.float32)
            for p in range(n):
                parts = [table[p, f].reshape(width, LANES) for f in range(lo, hi)]
                rhs = parts[0] if len(parts) == 1 else jnp.concatenate(parts, axis=1)
                total += dot_f32(onehot[p, pl.ds(first, cap), :], rhs)
            for f in range(lo, hi):
                out[f, e] = total[:, (f - lo) * LANES : (f - lo + 1) * LANES].astype(jnp.bfloat16)
            return carry

        lax.fori_loop(0, experts, body, 0)

    def send_away(lo, hi):
        select(lo, hi, 1, pick_send)
        for f in range(lo, min(hi, units)):
            pick_copy(f).start()

    def pick_here(lo, hi):
        select(lo, hi, 0, pick_own)

    def merge(unit):
        if unit < units:
            pick_copy(unit).wait_recv()
            far = unit >= slices
            owner = apart_chip(unit - slices) if far else chip
            f = rounds if far else unit
            picked[owner, f] = pick_own[unit] + pick_recv[unit]
            if unit <= slices:
                chip_start(f, 1)

    def multiply(f, first=False):
        def body(e, carry):
            total = jnp.zeros((cap, LANES), jnp.float32) if first else back[e]
            for y in range(ny):
                col = (y * feats + f) * LANES
                total += lax.dot_general(
                    picked[y, f, e],
                    w_buf[e, :, col : col + LANES],
                    (((1,), (1,)), ((), ())),
                    preferred_element_type=jnp.float32,
                )
            back[e] = total
            return carry

        lax.fori_loop(0, experts, body, 0)

    line_start(0)
    ids_copy().start()
    line_start(1)
    build_onehot(0)
    ids_copy().wait_recv()
    build_onehot(1)
    build_low_hot()
    line_wait(0)
    wide_start(0)
    line_wait(1)
    slab_start()
    wide_start(1)
    wide_start(2)
    ring_start(0, 1)
    slab_wait(1, 2)
    ring_start(1, 1)
    wide_wait(0)
    send_away(0, 1)
    pick_here(0, 1)
    merge(0)
    wide_wait(1)
    send_away(1, 2)
    pick_here(1, 2)
    merge(1)
    chip_go(0, 1)
    wide_wait(2)
    slab_wait(3, 4, 5)
    ring_start(2, 1)
    send_away(2, 3)
    chip_go(1, 1)
    pick_here(2, 3)
    ring_go(0, 1)
    merge(2)
    ring_go(1, 1)
    chip_go(0, 2)
    ring_go(2, 1)
    ring_go(0, 2)
    chip_go(1, 2)
    ring_go(1, 2)
    chip_go(2, 1)
    ring_go(2, 2)
    ring_go(0, 3)
    chip_go(0, 3)
    ring_go(1, 3)
    chip_go(1, 3)
    ring_go(2, 3)
    ring_go(0, 4)
    send_away(3, 5)
    ring_go(1, 4)
    pick_here(3, 5)
    chip_go(2, 2)
    send_away(5, 7)
    merge(4)
    pick_here(5, 7)
    chip_go(0, 4)
    ring_go(2, 4)
    send_away(7, 9)
    chip_go(1, 4)
    pick_here(7, 9)
    send_away(9, 10)
    pick_here(9, 10)
    chip_go(2, 3)
    merge(5)
    merge(6)
    merge(7)
    merge(8)
    merge(9)
    for load in loads[3:]:
        load.wait()
    multiply(0, True)
    multiply(1)
    pick_copy(scores).wait_recv()
    chip_go(3, 1)
    multiply(rounds)
    chip_go(2, 4)
    multiply(2)

    for e in range(experts):
        for b in range(cap // LANES):
            rows = slice(b * LANES, (b + 1) * LANES)
            g = gate_buf[e, rows, :].astype(jnp.float32)
            u = up_buf[e, rows, :].astype(jnp.float32)
            bk = back[e, rows, :]
            s = 1.0 / (1.0 + jnp.exp(-g))
            silu = g * s
            row = ids[0, e : e + 1, b * LANES : (b + 1) * LANES]
            place = jnp.transpose(jnp.broadcast_to(row, (LANES, LANES))) & ((1 << TOP_BITS) - 1)
            lane = lax.broadcasted_iota(jnp.int32, (LANES, LANES), 1)
            spread = pick_own[scores, e, rows, :].astype(jnp.float32) + pick_recv[
                scores, e, rows, :
            ].astype(jnp.float32)
            weight = jnp.sum(jnp.where(place == lane, spread, 0.0), axis=1, keepdims=True)
            product = silu * u * bk
            at = e * (cap // LANES) + b
            sums[chip, at : at + 1, :] = jnp.sum(jnp.transpose(product), axis=0, keepdims=True)
            scaled = weight * bk
            grad_gate_ref[e, rows, :] = (scaled * u * (s * (1.0 + g * (1.0 - s)))).astype(jnp.bfloat16)
            grad_up_ref[e, rows, :] = (scaled * silu).astype(jnp.bfloat16)

    def sum_copy(d, slot):
        return remote(
            sums.at[slot], sums.at[slot], sum_send.at[d], sum_recv.at[slot], node, lax.rem(chip + d, ny)
        )

    for d in range(1, ny):
        sum_copy(d, chip).start()
    for d in range(1, ny):
        sum_copy(d, lax.rem(chip + d, ny)).wait_recv()
    full = sums[0]
    for y in range(1, ny):
        full = full + sums[y]

    targets = 2 * n
    pieces = []
    for e in range(experts):
        for b in range(cap // LANES):
            at = e * (cap // LANES) + b
            row_node = ids[0, e : e + 1, b * LANES : (b + 1) * LANES] >> (TOP_BITS + bits_of(tokens))
            row_z = (row_node >> 1) & (n - 1)
            row_x = row_node >> (1 + nbits)
            row_target = jnp.where(
                ((row_z - z) & (n - 1)) == chip, row_x * 2 + (row_node & 1), -1
            )
            target = lax.broadcasted_iota(jnp.int32, (targets, LANES), 0)
            pieces.append(jnp.where(row_target == target, full[at : at + 1, :], 0.0))
    spread = jnp.concatenate(pieces, axis=1)
    high = spread.astype(jnp.bfloat16)
    rest = spread - high.astype(jnp.float32)
    middle = rest.astype(jnp.bfloat16)
    low = (rest - middle.astype(jnp.float32)).astype(jnp.bfloat16)
    dense = dot_f32(high, low_hot[...]) + dot_f32(middle, low_hot[...]) + dot_f32(low, low_hot[...])
    for i in range(targets):
        dense_send[i, 0:1, :] = dense[i : i + 1, :LANES]
        dense_send[i, 1:2, :] = dense[i : i + 1, LANES:]

    mine = 2 * x + core

    def dense_node(i, shift):
        return ((i // 2) * n + lax.rem(z + shift, n)) * 2 + lax.rem(i, 2)

    def dense_copy(i, slot, to):
        return remote(
            dense_send.at[i], dense_recv.at[slot], dense_send_sem.at[i], dense_recv_sem.at[slot], to, chip
        )

    def each_target(act, shift):
        def body(i, carry):
            to = dense_node(i, shift)

            @pl.when(to != node)
            def _():
                act(i, to)

            return carry

        lax.fori_loop(0, targets, body, 0)

    each_target(lambda i, to: dense_copy(i, mine, to).start(), chip)

    @pl.when(chip == 0)
    def _():
        dense_recv[mine] = dense_send[mine]

    each_target(lambda i, to: dense_copy(i, i, to).wait_recv(), n - chip)
    totals[chip] = jnp.sum(dense_recv[...], axis=0)

    def total_copy(d, slot):
        return remote(
            totals.at[slot], totals.at[slot], total_send.at[d], total_recv.at[slot], node, lax.rem(chip + d, ny)
        )

    for d in range(1, ny):
        total_copy(d, chip).start()
    for d in range(1, ny):
        total_copy(d, lax.rem(chip + d, ny)).wait_recv()
    grad_score_ref[...] = jnp.sum(totals[...], axis=0)

    each_target(lambda i, to: dense_copy(i, mine, to).wait_send(), chip)
    ids_copy().wait_send()
    for d in range(1, n):
        for f in range(rounds):
            wide_push(f, d).wait_send()
        for g in range(2):
            line_push(g, d).wait_send()
    for g in range(len(rings)):
        for s in range(1, half_ring + 1):
            for way in range(2):
                ring_copy(g, way, s, False).wait_send()
    for u in range(units):
        pick_copy(u).wait_send()
    for f in range(feats):
        for s in range(1, last_step(f) + 1):
            for way in range(2):
                chip_copy(f, way, s, False).wait_send()
    for i in range(1, len(apart)):
        slab_copy(i, False).wait_send()
    for d in range(1, ny):
        sum_copy(d, chip).wait_send()
        total_copy(d, chip).wait_send()


def on_device(n, ny, grad_out, route_score, expert_routes, expert_count, gate_pre, up_pre, w_down):
    tokens, features = grad_out.shape
    experts, cap = expert_routes.shape
    hidden = gate_pre.shape[2]
    feats = features // LANES
    units = feats + len(far_chips(ny))
    slots = experts * cap
    targets = 2 * n
    half_ring, half_chip = max(n // 2, 1), max(ny // 2, 1)
    bf16, f32 = jnp.bfloat16, jnp.float32
    dma = pltpu.SemaphoreType.DMA
    vmem = pl.BlockSpec(memory_space=pltpu.VMEM)
    hbm = pl.BlockSpec(memory_space=pltpu.HBM)
    grad_gate, grad_up, score = pl.pallas_call(
        functools.partial(kernel, n, ny),
        out_shape=(
            jax.ShapeDtypeStruct(gate_pre.shape, bf16),
            jax.ShapeDtypeStruct(gate_pre.shape, bf16),
            jax.ShapeDtypeStruct((2, LANES), f32),
        ),
        in_specs=[hbm, vmem, hbm, hbm, hbm, hbm, hbm],
        out_specs=(vmem, vmem, vmem),
        scratch_shapes=[
            pltpu.VMEM(grad_out.shape, bf16),
            pltpu.VMEM(expert_routes.shape, jnp.int32),
            pltpu.SMEM(expert_count.shape, jnp.int32),
            pltpu.VMEM((n, units, n, tokens, LANES), bf16),
            pltpu.VMEM((n, 2 * slots, n * tokens), bf16),
            pltpu.VMEM((2, experts, cap), jnp.int32),
            pltpu.VMEM((units, experts, cap, LANES), bf16),
            pltpu.VMEM((units, experts, cap, LANES), bf16),
            pltpu.VMEM((units, experts, cap, LANES), bf16),
            pltpu.VMEM((ny, feats, experts, cap, LANES), bf16),
            pltpu.VMEM(gate_pre.shape, bf16),
            pltpu.VMEM(up_pre.shape, bf16),
            pltpu.VMEM(w_down.shape, bf16),
            pltpu.VMEM((experts, cap, hidden), f32),
            pltpu.VMEM((slots, 2 * LANES), bf16),
            pltpu.VMEM((ny, slots // LANES, LANES), f32),
            pltpu.VMEM((targets, 2, LANES), f32),
            pltpu.VMEM((targets, 2, LANES), f32),
            pltpu.VMEM((ny, 2, LANES), f32),
            dma((6,)),
            dma,
            dma,
            dma((2, n)),
            dma((2, n)),
            dma((len(far_chips(ny)),)),
            dma((len(far_chips(ny)),)),
            dma((feats - 1, n)),
            dma((feats - 1, n)),
            dma((4, 2, half_ring)),
            dma((4, 2, half_ring)),
            dma((units,)),
            dma((units,)),
            dma((feats, 2, half_chip)),
            dma((feats, 2, half_chip)),
            dma((ny,)),
            dma((ny,)),
            dma((targets,)),
            dma((targets,)),
            dma((ny,)),
            dma((ny,)),
        ],
        compiler_params=pltpu.CompilerParams(
            collective_id=0, has_side_effects=True, vmem_limit_bytes=63 * 1024 * 1024
        ),
        name="expert_backward",
    )(grad_out, route_score.T, expert_routes, expert_count, gate_pre, up_pre, w_down)
    return grad_gate, grad_up, score.reshape(tokens, -1)


def solution(mesh):
    ny = mesh.shape["chip"]
    n = 1
    while 2 * n * n < mesh.shape["node"]:
        n *= 2
    placed = (
        P("node", "chip"),
        P("node", None),
        P("node", None),
        P("node"),
        P("node", None, "chip"),
        P("node", None, "chip"),
        P("node", "chip", None),
    )
    return jax.shard_map(
        functools.partial(on_device, n, ny),
        mesh=mesh,
        in_specs=placed,
        out_specs=(P("node", None, "chip"), P("node", None, "chip"), P("node", None)),
        check_vma=False,
    )
```

```python
import functools

import jax
import jax.numpy as jnp
from jax import lax
from jax.experimental import pallas as pl
from jax.experimental.pallas import tpu as pltpu
from jax.sharding import PartitionSpec as P

LANES = 128
TOP_BITS = 3
NEAR = 1


def bits_of(size):
    return size.bit_length() - 1


def dot_f32(a, b):
    return jnp.dot(a, b, preferred_element_type=jnp.float32)


def near_steps(ny):
    return max(min(NEAR, ny // 2 - 1), 0)


def far_chips(ny):
    apart = [0]
    for d in range(near_steps(ny) + 1, ny // 2):
        apart += [d, -d]
    return apart + [ny // 2]


def in_hbm(array):
    return pltpu.with_memory_space_constraint(array, pltpu.HBM)


def remote(src, dst, send, recv, node, chip):
    return pltpu.make_async_remote_copy(
        src_ref=src,
        dst_ref=dst,
        send_sem=send,
        recv_sem=recv,
        device_id=(node, chip),
        device_id_type=pl.DeviceIdType.MESH,
    )


def kernel(
    n,
    ny,
    grad_hbm,
    score_ref,
    routes_hbm,
    count_hbm,
    gate_hbm,
    up_hbm,
    w_hbm,
    grad_gate_ref,
    grad_up_ref,
    grad_score_ref,
    grad_ref,
    routes_ref,
    count_ref,
    table,
    onehot,
    ids,
    pick_send,
    pick_recv,
    pick_own,
    picked,
    gate_buf,
    up_buf,
    w_buf,
    back,
    low_hot,
    sums,
    dense_send,
    dense_recv,
    totals,
    in_sem,
    ids_send_sem,
    ids_recv_sem,
    line_send,
    line_recv,
    slab_send,
    slab_recv,
    wide_send,
    wide_recv,
    ring_send,
    ring_recv,
    pick_send_sem,
    pick_recv_sem,
    chip_send,
    chip_recv,
    sum_send,
    sum_recv,
    dense_send_sem,
    dense_recv_sem,
    total_send,
    total_recv,
):
    units = table.shape[1]
    tokens = table.shape[3]
    experts, cap = routes_ref.shape
    slots = experts * cap
    width = n * tokens
    half_ring, half_chip = n // 2, ny // 2
    nbits = bits_of(n)
    feats = w_buf.shape[2] // (ny * LANES)
    rounds = feats - 1
    scores, slices = rounds, rounds + 1
    reach = near_steps(ny)
    apart = far_chips(ny)
    pushes = ((0, 1), (1, slices + 1))
    rings = [(scores, slices + 1)]
    for lo in range(slices + 1, max(units - 1, slices + 2), 2):
        rings.append((lo, units if lo + 3 >= units else lo + 2))

    def last_step(f):
        return reach if f == rounds else half_chip

    node = lax.axis_index("node")
    chip = lax.axis_index("chip")
    core = lax.rem(node, 2)
    z = lax.rem(node // 2, n)
    x = node // (2 * n)
    line = x + core * (z - x)
    ring = z + core * (x - z)
    sibling = node + 1 - 2 * core

    def node_at(ring_pos, line_pos):
        at_x = line_pos + core * (ring_pos - line_pos)
        at_z = ring_pos + core * (line_pos - ring_pos)
        return (at_x * n + at_z) * 2 + core

    def line_peer(d):
        return lax.rem(line + d, n)

    loads = [
        pltpu.make_async_copy(src, dst, in_sem.at[i])
        for i, (src, dst) in enumerate(
            (
                (grad_hbm, grad_ref),
                (routes_hbm, routes_ref),
                (count_hbm, count_ref),
                (w_hbm, w_buf),
                (gate_hbm, gate_buf),
                (up_hbm, up_buf),
            )
        )
    ]
    for load in loads:
        load.start()

    barrier = pltpu.get_barrier_semaphore()
    greeted = [(sibling, chip)]
    greeted += [(node_at(ring, line_peer(d)), chip) for d in range(1, n)]
    greeted += [(node_at(lax.rem(ring + d, n), line), chip) for d in range(1, n)]
    greeted += [(node, lax.rem(chip + d, ny)) for d in range(1, ny)]
    for peer in greeted:
        pl.semaphore_signal(
            barrier, inc=1, device_id=peer, device_id_type=pl.DeviceIdType.MESH
        )

    for load in loads[:3]:
        load.wait()
    for f in range(rounds):
        table[ring, f, line] = grad_ref[:, f * LANES : (f + 1) * LANES]
    table[ring, slices, line] = grad_ref[:, rounds * LANES : feats * LANES]
    tops = score_ref.shape[0]
    padded = jnp.concatenate(
        [score_ref[...].astype(jnp.float32), jnp.zeros((tops, LANES - tokens), jnp.float32)], axis=1
    )
    padded = jnp.concatenate([padded, jnp.zeros((LANES - tops, LANES), jnp.float32)], axis=0)
    table[ring, scores, line] = jnp.transpose(padded)[:tokens].astype(jnp.bfloat16)
    slot_lane = lax.broadcasted_iota(jnp.int32, (1, cap), 1)
    for e in range(experts):
        ids[0, e : e + 1, :] = jnp.where(
            slot_lane < count_ref[e], routes_ref[e : e + 1, :], -1
        )
    pl.semaphore_wait(barrier, len(greeted))

    def ids_copy():
        return remote(ids.at[0], ids.at[1], ids_send_sem, ids_recv_sem, sibling, chip)

    far_first = sorted(range(1, n), key=lambda d: -min(d, n - d))

    def line_push(g, d):
        lo, hi = pushes[g]
        block = table.at[ring, lo:hi, line]
        return remote(
            block, block, line_send.at[g, d], line_recv.at[g, line], node_at(ring, line_peer(d)), chip
        )

    def line_start(g):
        for d in far_first:
            line_push(g, d).start()

    def line_wait(g):
        lo, hi = pushes[g]
        for d in range(1, n):
            peer = line_peer(d)
            block = table.at[ring, lo:hi, peer]
            remote(
                block, block, line_send.at[g, d], line_recv.at[g, peer], node_at(ring, peer), chip
            ).wait_recv()

    def apart_chip(i):
        return lax.rem(chip + apart[i] + ny, ny)

    def slab_copy(i, arrival):
        back_i = i if apart[i] == half_chip else apart.index(-apart[i])
        mine = table.at[ring, slices]
        if arrival:
            block = table.at[ring, slices + i]
            return remote(block, block, slab_send.at[i], slab_recv.at[i], node, apart_chip(i))
        there = table.at[ring, slices + back_i]
        return remote(mine, there, slab_send.at[i], slab_recv.at[back_i], node, apart_chip(i))

    def slab_start():
        for i in range(1, len(apart)):
            slab_copy(i, False).start()

    def slab_wait(*which):
        for i in which:
            if i < len(apart):
                slab_copy(i, True).wait_recv()

    def wide_push(f, d):
        block = table.at[ring, f]
        peer = lax.rem(ring + d, n)
        return remote(
            block, block, wide_send.at[f, d], wide_recv.at[f, ring], node_at(peer, line), chip
        )

    def wide_start(f):
        for d in far_first:
            wide_push(f, d).start()

    def wide_wait(f):
        for d in range(1, n):
            peer = lax.rem(ring + d, n)
            block = table.at[peer, f]
            remote(
                block, block, wide_send.at[f, d], wide_recv.at[f, peer], node_at(peer, line), chip
            ).wait_recv()

    def ring_block(g, way, s, pos):
        lo, hi = rings[g]
        if s < half_ring:
            return table.at[pos, lo:hi]
        return table.at[pos, lo:hi, pl.ds(way * half_ring, half_ring)]

    def ring_copy(g, way, s, arrival):
        step = 1 if way == 0 else n - 1
        hop = s if arrival else s - 1
        pos = lax.rem(ring + (n - step) * hop, n)
        block = ring_block(g, way, s, pos)
        to = node_at(lax.rem(ring + step, n), line)
        return remote(block, block, ring_send.at[g, way, s - 1], ring_recv.at[g, way, s - 1], to, chip)

    def ring_start(g, s):
        if g < len(rings):
            for way in range(2):
                ring_copy(g, way, s, False).start()

    def ring_go(g, s):
        if g < len(rings) and s <= half_ring:
            for way in range(2):
                ring_copy(g, way, s, True).wait_recv()
            if s < half_ring:
                ring_start(g, s + 1)

    def chip_copy(f, way, s, arrival):
        step = 1 if way == 0 else ny - 1
        hop = s if arrival else s - 1
        pos = lax.rem(chip + (ny - step) * hop, ny)
        block = picked.at[pos, f] if s < half_chip else picked.at[pos, f, pl.ds(way * (experts // 2), experts // 2)]
        to = lax.rem(chip + step, ny)
        return remote(block, block, chip_send.at[f, way, s - 1], chip_recv.at[f, way, s - 1], node, to)

    def chip_start(f, s):
        if s <= last_step(f):
            for way in range(2):
                chip_copy(f, way, s, False).start()

    def chip_go(f, s):
        if s <= last_step(f):
            for way in range(2):
                chip_copy(f, way, s, True).wait_recv()
            chip_start(f, s + 1)

    def pick_copy(f):
        return remote(
            pick_send.at[f], pick_recv.at[f], pick_send_sem.at[f], pick_recv_sem.at[f], sibling, chip
        )

    def build_onehot(side):
        lanes = min(width, LANES)
        for e in range(experts):
            for b in range(cap // LANES):
                row = ids[side, e : e + 1, b * LANES : (b + 1) * LANES]
                col = jnp.transpose(jnp.broadcast_to(row, (LANES, LANES)))[:, :lanes]
                col_node = col >> (TOP_BITS + bits_of(tokens))
                col_core = col_node & 1
                col_z = (col_node >> 1) & (n - 1)
                col_x = col_node >> (1 + nbits)
                col_line = col_x + core * (col_z - col_x)
                col_ring = col_z + core * (col_x - col_z)
                inner = (col >> TOP_BITS) & (tokens - 1)
                key = col_ring * width + col_line * tokens + inner
                key = jnp.where((col >= 0) & (col_core == core), key, -1)
                key = key - lax.broadcasted_iota(jnp.int32, (LANES, lanes), 1)
                first = (side * experts + e) * cap + b * LANES

                def body(p, carry):
                    for h in range(width // lanes):
                        hit = key == p * width + h * lanes
                        onehot[p, first : first + LANES, h * lanes : (h + 1) * lanes] = jnp.where(
                            hit, 1.0, 0.0
                        ).astype(jnp.bfloat16)
                    return carry

                lax.fori_loop(0, n, body, 0)

    def build_low_hot():
        lane = lax.broadcasted_iota(jnp.int32, (LANES, 2 * LANES), 1)
        for e in range(experts):
            for b in range(cap // LANES):
                row = ids[0, e : e + 1, b * LANES : (b + 1) * LANES]
                col = jnp.transpose(jnp.broadcast_to(row, (2 * LANES, LANES)))
                first = e * cap + b * LANES
                low_hot[first : first + LANES, :] = jnp.where(
                    (col & (2 * LANES - 1)) == lane, 1.0, 0.0
                ).astype(jnp.bfloat16)

    def select(lo, hi, side, out):
        hi = min(hi, units)
        if lo >= hi:
            return

        def body(e, carry):
            first = pl.multiple_of((side * experts + e) * cap, cap)
            total = jnp.zeros((cap, (hi - lo) * LANES), jnp.float32)
            for p in range(n):
                parts = [table[p, f].reshape(width, LANES) for f in range(lo, hi)]
                rhs = parts[0] if len(parts) == 1 else jnp.concatenate(parts, axis=1)
                total += dot_f32(onehot[p, pl.ds(first, cap), :], rhs)
            for f in range(lo, hi):
                out[f, e] = total[:, (f - lo) * LANES : (f - lo + 1) * LANES].astype(jnp.bfloat16)
            return carry

        lax.fori_loop(0, experts, body, 0)

    def send_away(lo, hi):
        select(lo, hi, 1, pick_send)
        for f in range(lo, min(hi, units)):
            pick_copy(f).start()

    def pick_here(lo, hi):
        select(lo, hi, 0, pick_own)

    def merge(unit):
        if unit < units:
            pick_copy(unit).wait_recv()
            far = unit >= slices
            owner = apart_chip(unit - slices) if far else chip
            f = rounds if far else unit
            picked[owner, f] = pick_own[unit] + pick_recv[unit]
            if unit <= slices:
                chip_start(f, 1)

    def multiply(f, first=False):
        def body(e, carry):
            total = jnp.zeros((cap, LANES), jnp.float32) if first else back[e]
            for y in range(ny):
                col = (y * feats + f) * LANES
                total += lax.dot_general(
                    picked[y, f, e],
                    w_buf[e, :, col : col + LANES],
                    (((1,), (1,)), ((), ())),
                    preferred_element_type=jnp.float32,
                )
            back[e] = total
            return carry

        lax.fori_loop(0, experts, body, 0)

    line_start(0)
    ids_copy().start()
    line_start(1)
    build_onehot(0)
    ids_copy().wait_recv()
    build_onehot(1)
    build_low_hot()
    line_wait(0)
    wide_start(0)
    line_wait(1)
    slab_start()
    wide_start(1)
    wide_start(2)
    ring_start(0, 1)
    slab_wait(1, 2)
    ring_start(1, 1)
    wide_wait(0)
    send_away(0, 1)
    pick_here(0, 1)
    merge(0)
    wide_wait(1)
    send_away(1, 2)
    pick_here(1, 2)
    merge(1)
    chip_go(0, 1)
    wide_wait(2)
    slab_wait(3, 4, 5)
    ring_start(2, 1)
    send_away(2, 3)
    chip_go(1, 1)
    pick_here(2, 3)
    ring_go(0, 1)
    merge(2)
    ring_go(1, 1)
    chip_go(0, 2)
    ring_go(2, 1)
    ring_go(0, 2)
    chip_go(1, 2)
    ring_go(1, 2)
    chip_go(2, 1)
    ring_go(2, 2)
    ring_go(0, 3)
    chip_go(0, 3)
    ring_go(1, 3)
    chip_go(1, 3)
    ring_go(2, 3)
    ring_go(0, 4)
    send_away(3, 5)
    ring_go(1, 4)
    pick_here(3, 5)
    chip_go(2, 2)
    send_away(5, 7)
    merge(4)
    pick_here(5, 7)
    chip_go(0, 4)
    ring_go(2, 4)
    send_away(7, 9)
    chip_go(1, 4)
    pick_here(7, 9)
    send_away(9, 10)
    pick_here(9, 10)
    chip_go(2, 3)
    merge(5)
    merge(6)
    merge(7)
    merge(8)
    merge(9)
    for load in loads[3:]:
        load.wait()
    multiply(0, True)
    multiply(1)
    pick_copy(scores).wait_recv()
    chip_go(3, 1)
    multiply(rounds)
    chip_go(2, 4)
    multiply(2)

    def hidden_parts(e, rows):
        g = gate_buf[e, rows, :].astype(jnp.float32)
        u = up_buf[e, rows, :].astype(jnp.float32)
        s = 1.0 / (1.0 + jnp.exp(-g))
        return g, u, s, g * s

    slot_rows = [slice(b * LANES, (b + 1) * LANES) for b in range(cap // LANES)]
    for e in range(experts):
        for b, rows in enumerate(slot_rows):
            g, u, s, silu = hidden_parts(e, rows)
            product = silu * u * back[e, rows, :]
            at = e * (cap // LANES) + b
            sums[chip, at : at + 1, :] = jnp.sum(jnp.transpose(product), axis=0, keepdims=True)

    def sum_copy(d, slot):
        return remote(
            sums.at[slot], sums.at[slot], sum_send.at[d], sum_recv.at[slot], node, lax.rem(chip + d, ny)
        )

    for d in range(1, ny):
        sum_copy(d, chip).start()

    for e in range(experts):
        for b, rows in enumerate(slot_rows):
            g, u, s, silu = hidden_parts(e, rows)
            row = ids[0, e : e + 1, b * LANES : (b + 1) * LANES]
            place = jnp.transpose(jnp.broadcast_to(row, (LANES, LANES))) & ((1 << TOP_BITS) - 1)
            lane = lax.broadcasted_iota(jnp.int32, (LANES, LANES), 1)
            spread = pick_own[scores, e, rows, :].astype(jnp.float32) + pick_recv[
                scores, e, rows, :
            ].astype(jnp.float32)
            weight = jnp.sum(jnp.where(place == lane, spread, 0.0), axis=1, keepdims=True)
            scaled = weight * back[e, rows, :]
            grad_gate_ref[e, rows, :] = (scaled * u * (s * (1.0 + g * (1.0 - s)))).astype(jnp.bfloat16)
            grad_up_ref[e, rows, :] = (scaled * silu).astype(jnp.bfloat16)

    ids_copy().wait_send()
    for d in range(1, n):
        for f in range(rounds):
            wide_push(f, d).wait_send()
        for g in range(2):
            line_push(g, d).wait_send()
    for g in range(len(rings)):
        for s in range(1, half_ring + 1):
            for way in range(2):
                ring_copy(g, way, s, False).wait_send()
    for u in range(units):
        pick_copy(u).wait_send()
    for f in range(feats):
        for s in range(1, last_step(f) + 1):
            for way in range(2):
                chip_copy(f, way, s, False).wait_send()
    for i in range(1, len(apart)):
        slab_copy(i, False).wait_send()

    for d in range(1, ny):
        sum_copy(d, lax.rem(chip + d, ny)).wait_recv()
    full = sums[0]
    for y in range(1, ny):
        full = full + sums[y]

    targets = 2 * n
    pieces = []
    for e in range(experts):
        for b in range(cap // LANES):
            at = e * (cap // LANES) + b
            row_node = ids[0, e : e + 1, b * LANES : (b + 1) * LANES] >> (TOP_BITS + bits_of(tokens))
            row_z = (row_node >> 1) & (n - 1)
            row_x = row_node >> (1 + nbits)
            row_target = jnp.where(
                ((row_z - z) & (n - 1)) == chip, row_x * 2 + (row_node & 1), -1
            )
            target = lax.broadcasted_iota(jnp.int32, (targets, LANES), 0)
            pieces.append(jnp.where(row_target == target, full[at : at + 1, :], 0.0))
    spread = jnp.concatenate(pieces, axis=1)
    high = spread.astype(jnp.bfloat16)
    rest = spread - high.astype(jnp.float32)
    middle = rest.astype(jnp.bfloat16)
    low = (rest - middle.astype(jnp.float32)).astype(jnp.bfloat16)
    dense = dot_f32(high, low_hot[...]) + dot_f32(middle, low_hot[...]) + dot_f32(low, low_hot[...])
    for i in range(targets):
        dense_send[i, 0:1, :] = dense[i : i + 1, :LANES]
        dense_send[i, 1:2, :] = dense[i : i + 1, LANES:]

    mine = 2 * x + core

    def dense_node(i, shift):
        return ((i // 2) * n + lax.rem(z + shift, n)) * 2 + lax.rem(i, 2)

    def dense_copy(i, slot, to):
        return remote(
            dense_send.at[i], dense_recv.at[slot], dense_send_sem.at[i], dense_recv_sem.at[slot], to, chip
        )

    def each_target(act, shift):
        def body(i, carry):
            to = dense_node(i, shift)

            @pl.when(to != node)
            def _():
                act(i, to)

            return carry

        lax.fori_loop(0, targets, body, 0)

    each_target(lambda i, to: dense_copy(i, mine, to).start(), chip)

    @pl.when(chip == 0)
    def _():
        dense_recv[mine] = dense_send[mine]

    for d in range(1, ny):
        sum_copy(d, chip).wait_send()
    each_target(lambda i, to: dense_copy(i, i, to).wait_recv(), n - chip)
    totals[chip] = jnp.sum(dense_recv[...], axis=0)

    def total_copy(d, slot):
        return remote(
            totals.at[slot], totals.at[slot], total_send.at[d], total_recv.at[slot], node, lax.rem(chip + d, ny)
        )

    for d in range(1, ny):
        total_copy(d, chip).start()
    each_target(lambda i, to: dense_copy(i, mine, to).wait_send(), chip)
    for d in range(1, ny):
        total_copy(d, lax.rem(chip + d, ny)).wait_recv()
    grad_score_ref[...] = jnp.sum(totals[...], axis=0)
    for d in range(1, ny):
        total_copy(d, chip).wait_send()


def on_device(n, ny, grad_out, route_score, expert_routes, expert_count, gate_pre, up_pre, w_down):
    tokens, features = grad_out.shape
    experts, cap = expert_routes.shape
    hidden = gate_pre.shape[2]
    feats = features // LANES
    units = feats + len(far_chips(ny))
    slots = experts * cap
    targets = 2 * n
    half_ring, half_chip = max(n // 2, 1), max(ny // 2, 1)
    bf16, f32 = jnp.bfloat16, jnp.float32
    dma = pltpu.SemaphoreType.DMA
    vmem = pl.BlockSpec(memory_space=pltpu.VMEM)
    hbm = pl.BlockSpec(memory_space=pltpu.HBM)
    grad_gate, grad_up, score = pl.pallas_call(
        functools.partial(kernel, n, ny),
        out_shape=(
            jax.ShapeDtypeStruct(gate_pre.shape, bf16),
            jax.ShapeDtypeStruct(gate_pre.shape, bf16),
            jax.ShapeDtypeStruct((2, LANES), f32),
        ),
        in_specs=[hbm, vmem, hbm, hbm, hbm, hbm, hbm],
        out_specs=(vmem, vmem, vmem),
        scratch_shapes=[
            pltpu.VMEM(grad_out.shape, bf16),
            pltpu.VMEM(expert_routes.shape, jnp.int32),
            pltpu.SMEM(expert_count.shape, jnp.int32),
            pltpu.VMEM((n, units, n, tokens, LANES), bf16),
            pltpu.VMEM((n, 2 * slots, n * tokens), bf16),
            pltpu.VMEM((2, experts, cap), jnp.int32),
            pltpu.VMEM((units, experts, cap, LANES), bf16),
            pltpu.VMEM((units, experts, cap, LANES), bf16),
            pltpu.VMEM((units, experts, cap, LANES), bf16),
            pltpu.VMEM((ny, feats, experts, cap, LANES), bf16),
            pltpu.VMEM(gate_pre.shape, bf16),
            pltpu.VMEM(up_pre.shape, bf16),
            pltpu.VMEM(w_down.shape, bf16),
            pltpu.VMEM((experts, cap, hidden), f32),
            pltpu.VMEM((slots, 2 * LANES), bf16),
            pltpu.VMEM((ny, slots // LANES, LANES), f32),
            pltpu.VMEM((targets, 2, LANES), f32),
            pltpu.VMEM((targets, 2, LANES), f32),
            pltpu.VMEM((ny, 2, LANES), f32),
            dma((6,)),
            dma,
            dma,
            dma((2, n)),
            dma((2, n)),
            dma((len(far_chips(ny)),)),
            dma((len(far_chips(ny)),)),
            dma((feats - 1, n)),
            dma((feats - 1, n)),
            dma((4, 2, half_ring)),
            dma((4, 2, half_ring)),
            dma((units,)),
            dma((units,)),
            dma((feats, 2, half_chip)),
            dma((feats, 2, half_chip)),
            dma((ny,)),
            dma((ny,)),
            dma((targets,)),
            dma((targets,)),
            dma((ny,)),
            dma((ny,)),
        ],
        compiler_params=pltpu.CompilerParams(
            collective_id=0, has_side_effects=True, vmem_limit_bytes=40 * 1024 * 1024
        ),
        name="expert_backward",
    )(
        in_hbm(grad_out),
        route_score.T,
        in_hbm(expert_routes),
        in_hbm(expert_count),
        in_hbm(gate_pre),
        in_hbm(up_pre),
        in_hbm(w_down),
    )
    return grad_gate, grad_up, score.reshape(tokens, -1)


def solution(mesh):
    ny = mesh.shape["chip"]
    n = 1
    while 2 * n * n < mesh.shape["node"]:
        n *= 2
    placed = (
        P("node", "chip"),
        P("node", None),
        P("node", None),
        P("node"),
        P("node", None, "chip"),
        P("node", None, "chip"),
        P("node", "chip", None),
    )
    return jax.shard_map(
        functools.partial(on_device, n, ny),
        mesh=mesh,
        in_specs=placed,
        out_specs=(P("node", None, "chip"), P("node", None, "chip"), P("node", None)),
        check_vma=False,
    )
```
